32 devices in a mesh: fsdp: 32 (over z, y, x, core).
Axes of the slice: x: 2, y: 2, z: 4, core: 2. Of those that a mesh axis runs over, the one named last changes fastest.
Arguments:
- tokens: bfloat16 [16384, 768], P('fsdp'), may hold values from -6 to 6
- lengths: int32 [12], replicated, may hold values from 1 to 2048, 12288 in all
- counts: int32 [32], replicated, may hold values from 256 to 512, as said below
- ln1_gain: bfloat16 [768], P('fsdp'), may hold values from 0.5 to 1.5
- ln1_bias: bfloat16 [768], P('fsdp'), may hold values from -1 to 1
- w_qkv: bfloat16 [768, 2304], P('fsdp'), may hold values from -0.3125 to 0.3125
- bias_q: bfloat16 [768], P('fsdp'), may hold values from -1 to 1
- bias_v: bfloat16 [768], P('fsdp'), may hold values from -1 to 1
- w_out: bfloat16 [768, 768], P('fsdp'), may hold values from -0.875 to 0.875
- bias_out: bfloat16 [768], P('fsdp'), may hold values from -1 to 1
- ln2_gain: bfloat16 [768], P('fsdp'), may hold values from 0.5 to 1.5
- ln2_bias: bfloat16 [768], P('fsdp'), may hold values from -1 to 1
- w_fc: bfloat16 [768, 3072], P('fsdp'), may hold values from -0.21875 to 0.21875
- bias_fc: bfloat16 [3072], P('fsdp'), may hold values from -1 to 1
- w_proj: bfloat16 [3072, 768], P('fsdp'), may hold values from -0.109375 to 0.109375
- bias_proj: bfloat16 [768], P('fsdp'), may hold values from -1 to 1
- grad_out: bfloat16 [16384, 768], P('fsdp'), may hold values from -6 to 6
Outputs:
- activations: bfloat16 [16384, 768], P('fsdp')
- grad_tokens: bfloat16 [16384, 768], P('fsdp')
- grad_ln1_gain: float32 [768], P('fsdp')
- grad_ln1_bias: float32 [768], P('fsdp')
- grad_w_qkv: float32 [768, 2304], P('fsdp')
- grad_bias_q: float32 [768], P('fsdp')
- grad_bias_v: float32 [768], P('fsdp')
- grad_w_out: float32 [768, 768], P('fsdp')
- grad_bias_out: float32 [768], P('fsdp')
- grad_ln2_gain: float32 [768], P('fsdp')
- grad_ln2_bias: float32 [768], P('fsdp')
- grad_w_fc: float32 [768, 3072], P('fsdp')
- grad_bias_fc: float32 [3072], P('fsdp')
- grad_w_proj: float32 [3072, 768], P('fsdp')
- grad_bias_proj: float32 [768], P('fsdp')
The draws below stay inside these ranges and needn't reach their ends.
Inputs may be any that keep to these rules, and one draw needn't show every extreme that they name: The lengths sum to 12288 and the largest is exactly 2048; the sequences lie one after another over the live slots in device order. Device i holds counts[i] live tokens in its first slots and empty slots after them; the counts sum to 12288; in every draw some device is full and some holds exactly 256.
All inputs are finite; a program needn't handle non-finite values.
Results may differ from the reference program's by a relative error of at most 0.017.
Values may be sent and summed in bfloat16 or wider, within the bound.
A program may use at most 320 MiB of HBM per device.

```python
import math
import jax
import jax.numpy as jnp
import numpy as np
from jax import lax

D = 768
H = 12
HD = 64
FF = 3072
TOK_DEV = 512
MAXLEN = 2048
RANGES = 32
TOKENS = 16384
LIVE = 12288
NSEQ = 12
REACH = 8


def draw_counts(key, part):
    key = jax.random.fold_in(key, 7)
    half = RANGES // 2
    quarter = TOK_DEV // 4
    spread = jax.random.randint(jax.random.fold_in(key, 1), (half,), 0, quarter + 1)
    first = jnp.arange(half, dtype=jnp.int32) == 0
    spread = jnp.where(first, quarter, spread)
    middle_count = 3 * quarter
    paired = jnp.stack([middle_count + spread, middle_count - spread], axis=1).reshape(RANGES)
    order = jax.random.permutation(jax.random.fold_in(key, 2), RANGES)
    return paired[order].astype(jnp.int32)


def shard_levels(own_key, shape, shards, low, top_value):
    def one(dim, blocks):
        steps = jax.random.uniform(jax.random.fold_in(jax.random.fold_in(own_key, 6), dim), (blocks,), jnp.float32, low / len(shards), top_value / len(shards))
        return jnp.repeat(jnp.exp(steps), shape[dim] // blocks).reshape((-1,) + (1,) * (len(shape) - dim - 1))

    loudness = one(*shards[0])
    for cut in shards[1:]:
        loudness = loudness * one(*cut)
    return loudness


def profile(count, total, most, slope):
    weights = [(1 << 20) // math.isqrt(standing ** slope) + 1 for standing in range(2, count + 1)]
    rest, given = total - most - (count - 1), [1] * (count - 1)
    while rest > 0:
        movable = [i for i in range(count - 1) if given[i] < most]
        pool, remaining = sum([weights[i] for i in movable]), rest
        for i in movable:
            addition = min(most - given[i], max(1, remaining * weights[i] // pool), rest)
            given[i] = given[i] + addition
            rest = rest - addition
    return np.array([most] + given)


def uneven_parts(stream_key, count, total, reach, slope):
    if count == 2:
        one = jax.random.randint(stream_key, (), max(1, total - reach), min(reach, total - 1) + 1)
        return jnp.stack([one, total - one])
    sizes = jnp.asarray(profile(count, total, reach, slope), jnp.int32)
    pairs = (count - 1) // 2
    giver, taker = sizes[1:1 + 2 * pairs:2], sizes[2:2 + 2 * pairs:2]
    slack = jnp.minimum(giver - 1, reach - taker)
    shifted = jax.random.randint(jax.random.fold_in(stream_key, 1), (pairs,), 0, 1 << 20) % (slack + 1)
    sizes = sizes.at[1:1 + 2 * pairs:2].set(giver - shifted).at[2:2 + 2 * pairs:2].set(taker + shifted)
    return sizes[jax.random.permutation(jax.random.fold_in(stream_key, 2), count)]


def bell_draw(rng, extent, scale, reach, pieces=(), held_as=jnp.bfloat16):
    entries = jax.random.normal(rng, extent, jnp.float32) * scale
    if len(pieces) > 0:
        entries = shard_levels(rng, extent, pieces, -0.22, 0.18) * entries
    return jnp.clip(entries, min=-reach, max=reach).astype(held_as)


def setup_inputs(seed: int = 0) -> dict:
    key_list = jax.random.split(jax.random.key(seed), 18)
    return {
        "tokens": bell_draw(key_list[0], (TOKENS, D), 1.0, 6.0, ((0, 32),)),
        "lengths": uneven_parts(key_list[1], NSEQ, LIVE, MAXLEN, 1).astype(jnp.int32),
        "counts": draw_counts(jax.random.fold_in(key_list[17], 71), 0),
        "ln1_gain": jnp.clip(1.0 + 0.1 * jax.random.normal(key_list[3], (D,), jnp.float32), 0.5, 1.5).astype(jnp.bfloat16),
        "ln1_bias": bell_draw(key_list[4], (D,), 0.2, 1.0, ((0, 32),)),
        "w_qkv": bell_draw(key_list[5], (D, 3 * D), (D // 2) ** -0.5, 0.3125, ((0, 32),)),
        "bias_q": bell_draw(key_list[6], (D,), 0.2, 1.0, ((0, 32),)),
        "bias_v": bell_draw(key_list[7], (D,), 0.2, 1.0, ((0, 32),)),
        "w_out": bell_draw(key_list[8], (D, D), (D // 16) ** -0.5, 0.875, ((0, 32),)),
        "bias_out": bell_draw(key_list[9], (D,), 0.2, 1.0, ((0, 32),)),
        "ln2_gain": jnp.clip(1.0 + 0.1 * jax.random.normal(key_list[10], (D,), jnp.float32), 0.5, 1.5).astype(jnp.bfloat16),
        "ln2_bias": bell_draw(key_list[11], (D,), 0.2, 1.0, ((0, 32),)),
        "w_fc": bell_draw(key_list[12], (D, FF), D ** -0.5, 0.21875, ((0, 32),)),
        "bias_fc": bell_draw(key_list[13], (FF,), 0.2, 1.0, ((0, 32),)),
        "w_proj": bell_draw(key_list[14], (FF, D), FF ** -0.5, 0.109375, ((0, 32),)),
        "bias_proj": bell_draw(key_list[15], (D,), 0.2, 1.0, ((0, 32),)),
        "grad_out": bell_draw(key_list[16], (TOKENS, D), 1.0, 6.0, ((0, 32),)),
    }


@jax.custom_vjp
def low(v):
    return lax.optimization_barrier(v.astype(jnp.bfloat16)).astype(jnp.float32)

@jax.custom_vjp
def low_back(v):
    return v

def low_keep(v):
    return (low(v), None)

def low_pass(kept, grad):
    return (grad,)

def back_keep(v):
    return (v, None)

def back_low(kept, grad):
    return (low(grad),)
low.defvjp(low_keep, low_pass)
low_back.defvjp(back_keep, back_low)
epsilon = 1e-05
masked_out = -1e+30
highest = lax.Precision.HIGHEST

def layer_norm(values, gain_row, shift_row):
    average = lax.optimization_barrier(jnp.mean(values, axis=-1, keepdims=True))
    centred = values - average
    variance = lax.optimization_barrier(jnp.mean(centred * centred, axis=-1, keepdims=True))
    return centred * lax.rsqrt(variance + epsilon) * gain_row + shift_row

def slot_layout(lengths, counts):
    seq_ends = jnp.cumsum(lengths).astype(jnp.int32)
    starts = (jnp.cumsum(counts) - counts).astype(jnp.int32)
    slots = jnp.arange(TOKENS, dtype=jnp.int32)
    owner = (slots // TOK_DEV).astype(jnp.int32)
    offset = (slots - owner * TOK_DEV).astype(jnp.int32)
    places = (starts[owner] + offset).astype(jnp.int32)
    live = offset < counts[owner]
    passed = lax.optimization_barrier(jnp.sum((places[:, None] >= seq_ends[None, :]).astype(jnp.int32), axis=1)).astype(jnp.int32)
    seq_ids = jnp.where(live, passed, -slots - 1).astype(jnp.int32)
    return (seq_ids, places, live)

def attention(query_rows, key_rows, value_rows, seq_ids, places):
    front = REACH * TOK_DEV
    window = front + TOK_DEV
    pad_keys = jnp.concatenate([jnp.zeros((front, D), jnp.float32), key_rows], axis=0)
    pad_values = jnp.concatenate([jnp.zeros((front, D), jnp.float32), value_rows], axis=0)
    pad_ids = jnp.concatenate([jnp.full((front,), -TOKENS - 1, jnp.int32), seq_ids])
    pad_places = jnp.concatenate([jnp.full((front,), -1, jnp.int32), places])

    def one_block(number):
        first_row = (number * TOK_DEV).astype(jnp.int32)
        query_heads = lax.dynamic_slice_in_dim(query_rows, first_row, TOK_DEV, 0).reshape(TOK_DEV, H, HD)
        key_heads = lax.dynamic_slice_in_dim(pad_keys, first_row, window, 0).reshape(window, H, HD)
        value_heads = lax.dynamic_slice_in_dim(pad_values, first_row, window, 0).reshape(window, H, HD)
        query_ids = lax.dynamic_slice_in_dim(seq_ids, first_row, TOK_DEV, 0)
        query_places = lax.dynamic_slice_in_dim(places, first_row, TOK_DEV, 0)
        key_ids = lax.dynamic_slice_in_dim(pad_ids, first_row, window, 0)
        key_places = lax.dynamic_slice_in_dim(pad_places, first_row, window, 0)
        allowed = (key_ids[None, :] == query_ids[:, None]) & (key_places[None, :] <= query_places[:, None])
        raw_scores = jnp.einsum('qhd,khd->hqk', query_heads, key_heads, precision=highest) * HD ** (-0.5)
        raw_scores = low_back(raw_scores)
        masked = jnp.where(allowed[None], raw_scores, masked_out)
        softmax_low = low(jax.nn.softmax(masked, axis=-1))
        attended = jnp.einsum('hqk,khd->qhd', softmax_low, value_heads, precision=highest)
        return attended.reshape(TOK_DEV, D)
    numbers = jnp.arange(TOKENS // TOK_DEV, dtype=jnp.int32)
    return lax.map(jax.checkpoint(one_block), numbers).reshape(TOKENS, D)

def reference(tokens, lengths, counts, ln1_gain, ln1_bias, w_qkv, bias_q, bias_v, w_out, bias_out, ln2_gain, ln2_bias, w_fc, bias_fc, w_proj, bias_proj, grad_out):
    seq_ids, places, live = slot_layout(lengths, counts)

    def forward(inputs, gain_one, shift_one, weight_qkv, query_bias, value_bias, weight_out, out_bias, gain_two, shift_two, weight_fc, fc_bias, weight_proj, proj_bias):
        normed_one = low(layer_norm(inputs, gain_one, shift_one))
        projected = jnp.dot(normed_one, weight_qkv, precision=highest)
        query_rows = low(low_back(projected[:, :D] + query_bias))
        key_rows = low(low_back(projected[:, D:2 * D]))
        value_rows = low(low_back(projected[:, 2 * D:] + value_bias))
        mixed = low(low_back(attention(query_rows, key_rows, value_rows, seq_ids, places)))
        branch = low_back(jnp.dot(mixed, weight_out, precision=highest) + out_bias)
        middle = inputs + branch
        normed_two = low(layer_norm(middle, gain_two, shift_two))
        hidden = low_back(jnp.dot(normed_two, weight_fc, precision=highest) + fc_bias)
        active = low(jax.nn.gelu(hidden, approximate=True))
        result = middle + low_back(jnp.dot(active, weight_proj, precision=highest) + proj_bias)
        return jnp.where(live[:, None], result, jnp.float32(0.0))
    floats = (tokens.astype(jnp.float32), ln1_gain.astype(jnp.float32), ln1_bias.astype(jnp.float32), w_qkv.astype(jnp.float32), bias_q.astype(jnp.float32), bias_v.astype(jnp.float32), w_out.astype(jnp.float32), bias_out.astype(jnp.float32), ln2_gain.astype(jnp.float32), ln2_bias.astype(jnp.float32), w_fc.astype(jnp.float32), bias_fc.astype(jnp.float32), w_proj.astype(jnp.float32), bias_proj.astype(jnp.float32))
    result, pullback = jax.vjp(forward, *floats)
    grads = pullback(grad_out.astype(jnp.float32))
    return (result.astype(jnp.bfloat16), grads[0].astype(jnp.bfloat16), grads[1], grads[2], grads[3], grads[4], grads[5], grads[6], grads[7], grads[8], grads[9], grads[10], grads[11], grads[12], grads[13])
```

```python
import jax
import jax.numpy as jnp
from jax import lax
from jax.experimental import pallas as pl
from jax.experimental.pallas import tpu as pltpu
from jax.sharding import PartitionSpec as P

HD = 64
MAXLEN = 2048
PAIR = 2 * HD
REACH = 8
CHIPS = REACH // 2 + 1
SPOTS = 2 * CHIPS

epsilon = 1e-05
masked_out = -1e30
VMEM_LIMIT = 44 * 1024 * 1024


def layer_norm(values, gain_row, shift_row):
    average = jnp.mean(values, axis=-1, keepdims=True)
    centred = values - average
    variance = jnp.mean(centred * centred, axis=-1, keepdims=True)
    return centred * lax.rsqrt(variance + epsilon) * gain_row + shift_row


def smooth_gelu(values):
    return jax.nn.gelu(values, approximate=True)


def matmul(first_op, second_op):
    return jnp.dot(first_op, second_op, preferred_element_type=jnp.float32)


def times_transposed(first_op, second_op):
    return lax.dot_general(
        first_op, second_op, (((1,), (1,)), ((), ())), preferred_element_type=jnp.float32
    )


def transposed_times(first_op, second_op):
    return lax.dot_general(
        first_op, second_op, (((0,), (0,)), ((), ())), preferred_element_type=jnp.float32
    )


def column_sums(values):
    return jnp.sum(values.astype(jnp.float32), axis=0)


def from_behind(x, by):
    peers = lax.axis_size("fsdp")
    pairs = [(i, i + by) for i in range(peers) if 0 <= i + by < peers]
    return lax.ppermute(x, "fsdp", pairs)


def swap(x, bit):
    peers = lax.axis_size("fsdp")
    return lax.ppermute(x, "fsdp", [(i, i ^ (1 << bit)) for i in range(peers)])


def halves(dtype):
    lane = lax.broadcasted_iota(jnp.int32, (1, PAIR), 1)
    first = (lane < HD).astype(jnp.float32)
    return first.astype(dtype), (1.0 - first).astype(dtype)


def gather_blocks(nb_ref, kv_refs, kv_s, rows):
    far = jnp.maximum(nb_ref[0], nb_ref[1] - 1)
    for e in range(CHIPS):
        low = (SPOTS - 2 - 2 * e) * rows

        def fill(e=e, low=low):
            kv_s[:, low : low + 2 * rows, :] = kv_refs[e][...]

        if e == 0:
            fill()
        else:
            pl.when(far >= 2 * e - 1)(fill)


def forward_kernel(nb_ref, q_ref, *refs):
    kv_refs = refs[:CHIPS]
    lo_ref, hi_ref, code_ref, o_ref, lse_ref, kv_s = refs[CHIPS:]
    rows = q_ref.shape[0] // 2
    gather_blocks(nb_ref, kv_refs, kv_s, rows)
    first, second = halves(jnp.bfloat16)
    first_f, second_f = halves(jnp.float32)
    for qb in range(2):
        q = q_ref[qb * rows : (qb + 1) * rows, :]
        q_heads = (q * first, q * second)
        lo, hi = lo_ref[qb], hi_ref[qb]

        def tile(d, carry, q_heads=q_heads, lo=lo, hi=hi, qb=qb):
            tops, totals, acc = carry
            spot = SPOTS - 2 + qb - d
            at = pl.ds(pl.multiple_of(spot * rows, rows), rows)
            k, v = kv_s[0, at, :], kv_s[1, at, :]
            code = code_ref[spot]
            ok = (code >= lo) & (code <= hi)
            new_tops, new_totals, decays = [], [], []
            gain = None
            for h, v_mask in enumerate((first, second)):
                s = jnp.where(ok, times_transposed(q_heads[h], k), masked_out)
                top = jnp.maximum(tops[h], jnp.max(s, axis=1, keepdims=True))
                p = jnp.exp(s - top)
                decay = jnp.exp(tops[h] - top)
                new_tops.append(top)
                new_totals.append(totals[h] * decay + jnp.sum(p, axis=1, keepdims=True))
                decays.append(decay)
                part = matmul(p.astype(jnp.bfloat16), v * v_mask)
                gain = part if gain is None else gain + part
            acc = acc * (decays[0] * first_f + decays[1] * second_f) + gain
            return tuple(new_tops), tuple(new_totals), acc

        start = jnp.full((rows, 1), masked_out, jnp.float32)
        none = jnp.zeros((rows, 1), jnp.float32)
        tops, totals, acc = lax.fori_loop(
            0,
            nb_ref[qb] + 1,
            tile,
            ((start, start), (none, none), jnp.zeros((rows, PAIR), jnp.float32)),
        )
        here = slice(qb * rows, (qb + 1) * rows)
        o_ref[here, :] = acc / (totals[0] * first_f + totals[1] * second_f)
        lse = [tops[h] + jnp.log(totals[h]) for h in range(2)]
        lse_ref[here, :] = lse[0] * first_f + lse[1] * second_f


def backward_kernel(nb_ref, q_ref, do_ref, *refs):
    kv_refs = refs[:CHIPS]
    lo_ref, hi_ref, code_ref, stat_ref, dq_ref, dkv_ref, kv_s, dk_s, dv_s = refs[CHIPS:]
    rows = q_ref.shape[0] // 2
    gather_blocks(nb_ref, kv_refs, kv_s, rows)
    dk_s[...] = jnp.zeros_like(dk_s)
    dv_s[...] = jnp.zeros_like(dv_s)
    first, second = halves(jnp.bfloat16)
    for qb in range(2):
        here = slice(qb * rows, (qb + 1) * rows)
        q, do = q_ref[here, :], do_ref[here, :]
        q_heads = (q * first, q * second)
        do_heads = (do * first, do * second)
        lo, hi = lo_ref[qb], hi_ref[qb]

        def tile(d, dq_parts, q_heads=q_heads, do_heads=do_heads, lo=lo, hi=hi, qb=qb, here=here):
            spot = SPOTS - 2 + qb - d
            at = pl.ds(pl.multiple_of(spot * rows, rows), rows)
            k, v = kv_s[0, at, :], kv_s[1, at, :]
            k_turned = k.astype(jnp.float32).T.astype(jnp.bfloat16)
            code = code_ref[spot]
            ok = (code >= lo) & (code <= hi)
            new_parts = []
            dk = dv = None
            for h in range(2):
                s = times_transposed(k, q_heads[h])
                p = jnp.where(ok, jnp.exp(s - stat_ref[h : h + 1, here]), 0.0)
                dp = times_transposed(v, do_heads[h])
                ds = (p * (dp - stat_ref[2 + h : 3 + h, here])).astype(jnp.bfloat16)
                dv_part = matmul(p.astype(jnp.bfloat16), do_heads[h])
                dk_part = matmul(ds, q_heads[h])
                dv = dv_part if dv is None else dv + dv_part
                dk = dk_part if dk is None else dk + dk_part
                new_parts.append(dq_parts[h] + matmul(k_turned[h * HD : (h + 1) * HD, :], ds))
            dk_s[at, :] += dk
            dv_s[at, :] += dv
            return tuple(new_parts)

        none = jnp.zeros((HD, rows), jnp.float32)
        parts = lax.fori_loop(0, nb_ref[qb] + 1, tile, (none, none))
        turned = jnp.concatenate(parts, axis=0).T
        dq_ref[here, :] = (turned * HD ** (-0.5)).astype(jnp.bfloat16)
    for e in range(CHIPS):
        low = (SPOTS - 2 - 2 * e) * rows
        dkv_ref[e, 0] = dk_s[low : low + 2 * rows, :].astype(jnp.bfloat16)
        dkv_ref[e, 1] = dv_s[low : low + 2 * rows, :].astype(jnp.bfloat16)


def specs(count):
    return [pl.BlockSpec(memory_space=pltpu.SMEM)] + [pl.BlockSpec(memory_space=pltpu.VMEM)] * (
        count - 1
    )


def attend(nb, q, kvs, lo, hi, code):
    both = q.shape[0]
    operands = (nb, q, *kvs, lo, hi, code)
    out = jax.ShapeDtypeStruct((both, PAIR), jnp.float32)
    return pl.pallas_call(
        forward_kernel,
        out_shape=(out, out),
        in_specs=specs(len(operands)),
        out_specs=(pl.BlockSpec(memory_space=pltpu.VMEM),) * 2,
        scratch_shapes=[pltpu.VMEM((2, CHIPS * both, PAIR), jnp.bfloat16)],
        compiler_params=pltpu.CompilerParams(vmem_limit_bytes=VMEM_LIMIT),
        cost_estimate=pl.CostEstimate(
            flops=8 * both * both * 3 * PAIR, bytes_accessed=8 * both * PAIR * 4, transcendentals=0
        ),
        name="attend",
    )(*operands)


def attend_back(nb, q, do, kvs, lo, hi, code, stats):
    both = q.shape[0]
    operands = (nb, q, do, *kvs, lo, hi, code, stats)
    return pl.pallas_call(
        backward_kernel,
        out_shape=(
            jax.ShapeDtypeStruct((both, PAIR), jnp.bfloat16),
            jax.ShapeDtypeStruct((CHIPS, 2, both, PAIR), jnp.bfloat16),
        ),
        in_specs=specs(len(operands)),
        out_specs=(pl.BlockSpec(memory_space=pltpu.VMEM),) * 2,
        scratch_shapes=[
            pltpu.VMEM((2, CHIPS * both, PAIR), jnp.bfloat16),
            pltpu.VMEM((CHIPS * both, PAIR), jnp.float32),
            pltpu.VMEM((CHIPS * both, PAIR), jnp.float32),
        ],
        compiler_params=pltpu.CompilerParams(vmem_limit_bytes=VMEM_LIMIT),
        cost_estimate=pl.CostEstimate(
            flops=20 * both * both * 3 * PAIR, bytes_accessed=16 * both * PAIR * 4, transcendentals=0
        ),
        name="attend_back",
    )(*operands)


def owner_sums(grads, device, order):
    peers = lax.axis_size("fsdp")
    levels = peers.bit_length() - 1
    width = grads.shape[1]
    held = grads.reshape((2,) * levels + (grads.shape[0] // peers, width))
    left = list(range(levels - 1, -1, -1))
    for bit in list(order) + list(range(len(order), levels)):
        axis = left.index(bit)
        own = (device >> bit) & 1
        sent = lax.dynamic_index_in_dim(held, 1 - own, axis, keepdims=False)
        kept = lax.dynamic_index_in_dim(held, own, axis, keepdims=False)
        held = kept + swap(sent.astype(jnp.bfloat16), bit).astype(jnp.float32)
        left.pop(axis)
    return held


def per_device(
    tokens,
    lengths,
    counts,
    ln1_gain,
    ln1_bias,
    w_qkv,
    bias_q,
    bias_v,
    w_out,
    bias_out,
    ln2_gain,
    ln2_bias,
    w_fc,
    bias_fc,
    w_proj,
    bias_proj,
    grad_out,
):
    rows, features = tokens.shape
    half = features // 2
    pair_count = half // PAIR
    peers = lax.axis_size("fsdp")
    device = lax.axis_index("fsdp")
    core = device % 2

    small_parts = (
        ln1_gain, ln1_bias, bias_q, bias_v, bias_out, ln2_gain, ln2_bias, bias_proj, bias_fc,
    )
    sizes = [part.shape[0] for part in small_parts]
    packed = jnp.concatenate(small_parts).reshape(1, -1)
    packed_all = lax.all_gather(packed, "fsdp", axis=0, tiled=True).astype(jnp.float32)
    weight_qkv = lax.all_gather(w_qkv, "fsdp", axis=0, tiled=True)
    weight_out = lax.all_gather(w_out, "fsdp", axis=0, tiled=True)
    weight_fc = lax.all_gather(w_fc, "fsdp", axis=0, tiled=True)
    weight_proj = lax.all_gather(w_proj, "fsdp", axis=0, tiled=True)
    whole, at = [], 0
    for size in sizes:
        whole.append(packed_all[:, at : at + size].reshape(-1))
        at += size
    (
        gain_one, shift_one, query_bias, value_bias, out_bias, gain_two, shift_two, proj_bias, fc_bias,
    ) = whole

    seq_ends = jnp.cumsum(lengths)
    seq_starts = seq_ends - lengths
    starts = jnp.cumsum(counts) - counts
    offsets = jnp.arange(rows, dtype=jnp.int32)
    total_slots = peers * rows

    def begin_of(places):
        passed = places[..., None] >= seq_ends
        nearest = jnp.max(jnp.where(passed, seq_ends, 0), axis=-1)
        return nearest

    def codes_of(owners):
        safe = jnp.clip(owners, 0, peers - 1)
        places = starts[safe][:, None] + offsets[None, :]
        alive = offsets[None, :] < counts[safe][:, None]
        blank = total_slots + safe[:, None] * rows + offsets[None, :]
        codes = jnp.where(alive, places, blank)
        return codes, jnp.where(alive, begin_of(places), blank)

    first_device = device - core
    near = first_device + jnp.arange(2, dtype=jnp.int32)
    around = first_device - (SPOTS - 2) + jnp.arange(SPOTS, dtype=jnp.int32)
    key_codes = codes_of(around)[0]
    hi, lo = codes_of(near)
    earliest = begin_of(starts[near])
    back = near[:, None] - jnp.arange(1, REACH + 1, dtype=jnp.int32)[None, :]
    back_safe = jnp.clip(back, 0, peers - 1)
    seen = (back >= 0) & (starts[back_safe] + counts[back_safe] > earliest[:, None])
    nb = jnp.sum(seen.astype(jnp.int32), axis=1)
    lo_col, hi_col, code_row = lo[:, :, None], hi[:, :, None], key_codes[:, None, :]
    lo_row, hi_row, code_col = lo[:, None, :], hi[:, None, :], key_codes[:, :, None]

    def trade(x):
        n = x.shape[0]
        cut = x.reshape(n, rows, 2, half)
        mine = lax.dynamic_index_in_dim(cut, core, 2, keepdims=False)
        other = swap(lax.dynamic_index_in_dim(cut, 1 - core, 2, keepdims=False), 0)
        low = jnp.where(core == 0, mine, other)
        high = jnp.where(core == 0, other, mine)
        return jnp.concatenate([low, high], axis=1)

    def trade_back(x):
        mine = lax.dynamic_slice_in_dim(x, core * rows, rows, 1)
        other = swap(lax.dynamic_slice_in_dim(x, (1 - core) * rows, rows, 1), 0)
        low = jnp.where(core == 0, mine, other)
        high = jnp.where(core == 0, other, mine)
        return jnp.concatenate([low, high], axis=2)

    live = (offsets < counts[device])[:, None]
    inputs = tokens.astype(jnp.float32)
    normed_low = layer_norm(inputs, gain_one, shift_one).astype(jnp.bfloat16)
    projected = matmul(normed_low, weight_qkv)
    query = (projected[:, :features] + query_bias).astype(jnp.bfloat16) * jnp.bfloat16(HD ** (-0.5))
    keys = projected[:, features : 2 * features].astype(jnp.bfloat16)
    vals = (projected[:, 2 * features :] + value_bias).astype(jnp.bfloat16)
    traded = trade(jnp.stack([query, keys, vals]))
    queries, blocks, outs, lses = [], [], [], []
    for pair in range(pair_count):
        columns = slice(pair * PAIR, (pair + 1) * PAIR)
        own = traded[1:, :, columns]
        queries.append(traded[0, :, columns])
        blocks.append([own] + [from_behind(own, 2 * e) for e in range(1, CHIPS)])
    for pair in range(pair_count):
        out, lse = attend(nb, queries[pair], blocks[pair], lo_col, hi_col, code_row)
        outs.append(out)
        lses.append(lse)
    attended = jnp.concatenate(outs, axis=1)
    mixed_low = trade_back(attended.astype(jnp.bfloat16)[None])[0]
    middle = inputs + matmul(mixed_low, weight_out) + out_bias
    two_low = layer_norm(middle, gain_two, shift_two).astype(jnp.bfloat16)
    hidden = matmul(two_low, weight_fc) + fc_bias
    active, gelu_back = jax.vjp(smooth_gelu, hidden)
    active_low = active.astype(jnp.bfloat16)
    result = middle + matmul(active_low, weight_proj) + proj_bias
    activations = jnp.where(live, result, 0.0).astype(jnp.bfloat16)

    upstream = jnp.where(live, grad_out.astype(jnp.float32), 0.0)
    upstream_low = upstream.astype(jnp.bfloat16)
    grad_w_proj = transposed_times(active_low, upstream_low)
    grad_bias_proj = jnp.sum(upstream, axis=0)
    d_active = times_transposed(upstream_low, weight_proj)
    d_hidden = gelu_back(d_active)[0].astype(jnp.bfloat16)
    grad_w_fc = transposed_times(two_low, d_hidden)
    grad_bias_fc = column_sums(d_hidden)
    d_normed_two = times_transposed(d_hidden, weight_fc)
    unused_two, norm_back_two = jax.vjp(layer_norm, middle, gain_two, shift_two)
    d_middle_part, grad_ln2_gain, grad_ln2_bias = norm_back_two(d_normed_two)
    d_middle = upstream + d_middle_part
    d_branch = d_middle.astype(jnp.bfloat16)
    grad_w_out = transposed_times(mixed_low, d_branch)
    grad_bias_out = column_sums(d_branch)
    d_attended = trade(times_transposed(d_branch, weight_out).astype(jnp.bfloat16)[None])[0]

    own_proj = owner_sums(grad_w_proj, device, (0, 1, 2))
    own_fc = owner_sums(grad_w_fc, device, (0, 2, 1))
    own_out = owner_sums(grad_w_out, device, (0, 2, 1))

    d_queries, d_pairs = [], []
    for pair in range(pair_count):
        columns = slice(pair * PAIR, (pair + 1) * PAIR)
        d_out = d_attended[:, columns]
        products = d_out.astype(jnp.float32) * outs[pair]
        delta = jnp.sum(products.reshape(2 * rows, 2, HD), axis=2)
        stats = jnp.concatenate([lses[pair][:, ::HD].T, delta.T], axis=0)
        d_query, d_blocks = attend_back(
            nb, queries[pair], d_out, blocks[pair], lo_row, hi_row, code_col, stats
        )
        total = d_blocks[0].astype(jnp.float32)
        for e in range(1, CHIPS):
            total = total + from_behind(d_blocks[e], -2 * e).astype(jnp.float32)
        d_queries.append(d_query)
        d_pairs.append(total.astype(jnp.bfloat16))
    d_heads = jnp.concatenate(
        [jnp.concatenate(d_queries, axis=1)[None], jnp.concatenate(d_pairs, axis=2)], axis=0
    )
    d_slots = trade_back(d_heads)
    d_projected = jnp.concatenate([d_slots[0], d_slots[1], d_slots[2]], axis=1)
    grad_w_qkv = transposed_times(normed_low, d_projected)
    own_qkv = owner_sums(grad_w_qkv, device, (0, 1, 2))
    grad_bias_q = column_sums(d_slots[0])
    grad_bias_v = column_sums(d_slots[2])
    d_normed_one = times_transposed(d_projected, weight_qkv)
    unused_one, norm_back_one = jax.vjp(layer_norm, inputs, gain_one, shift_one)
    d_input_part, grad_ln1_gain, grad_ln1_bias = norm_back_one(d_normed_one)
    grad_tokens = (d_middle + d_input_part).astype(jnp.bfloat16)

    small_grads = (
        grad_ln1_gain, grad_ln1_bias, grad_bias_q, grad_bias_v, grad_bias_out, grad_ln2_gain,
        grad_ln2_bias, grad_bias_proj, grad_bias_fc,
    )
    packed_grads = jnp.concatenate([g.reshape(peers, -1) for g in small_grads], axis=1)
    own_small = lax.psum_scatter(packed_grads, "fsdp", scatter_dimension=0, tiled=True)[0]
    small, at = [], 0
    for size in sizes:
        small.append(own_small[at : at + size])
        at += size
    (
        own_gain_one, own_shift_one, own_bias_q, own_bias_v, own_bias_out, own_gain_two,
        own_shift_two, own_bias_proj, own_bias_fc,
    ) = small
    return (
        activations,
        grad_tokens,
        own_gain_one,
        own_shift_one,
        own_qkv,
        own_bias_q,
        own_bias_v,
        own_out,
        own_bias_out,
        own_gain_two,
        own_shift_two,
        own_fc,
        own_bias_fc,
        own_proj,
        own_bias_proj,
    )


def solution(mesh):
    split_rows, split_flat = P("fsdp", None), P("fsdp")
    return jax.shard_map(
        per_device,
        mesh=mesh,
        in_specs=(
            split_rows, P(), P(),
            split_flat, split_flat, split_rows, split_flat, split_flat, split_rows, split_flat,
            split_flat, split_flat, split_rows, split_flat, split_rows, split_flat, split_rows,
        ),
        out_specs=(
            split_rows, split_rows,
            split_flat, split_flat, split_rows, split_flat, split_flat, split_rows, split_flat,
            split_flat, split_flat, split_rows, split_flat, split_rows, split_flat,
        ),
        check_vma=False,
    )
```

```python
import jax
import jax.numpy as jnp
from jax import lax
from jax.experimental import pallas as pl
from jax.experimental.pallas import tpu as pltpu
from jax.sharding import PartitionSpec as P

HD = 64
MAXLEN = 2048
PAIR = 2 * HD
REACH = 8
CHIPS = REACH // 2 + 1
SPOTS = 2 * CHIPS

epsilon = 1e-05
masked_out = -1e30
VMEM_LIMIT = 44 * 1024 * 1024


def layer_norm(values, gain_row, shift_row):
    average = jnp.mean(values, axis=-1, keepdims=True)
    centred = values - average
    variance = jnp.mean(centred * centred, axis=-1, keepdims=True)
    return centred * lax.rsqrt(variance + epsilon) * gain_row + shift_row


def smooth_gelu(values):
    return jax.nn.gelu(values, approximate=True)


def matmul(first_op, second_op):
    return jnp.dot(first_op, second_op, preferred_element_type=jnp.float32)


def times_transposed(first_op, second_op):
    return lax.dot_general(
        first_op, second_op, (((1,), (1,)), ((), ())), preferred_element_type=jnp.float32
    )


def transposed_times(first_op, second_op):
    return lax.dot_general(
        first_op, second_op, (((0,), (0,)), ((), ())), preferred_element_type=jnp.float32
    )


def column_sums(values):
    return jnp.sum(values.astype(jnp.float32), axis=0)


def from_behind(x, by):
    peers = lax.axis_size("fsdp")
    pairs = [(i, i + by) for i in range(peers) if 0 <= i + by < peers]
    return lax.ppermute(x, "fsdp", pairs)


def swap(x, bit):
    peers = lax.axis_size("fsdp")
    return lax.ppermute(x, "fsdp", [(i, i ^ (1 << bit)) for i in range(peers)])


def halves(dtype):
    lane = lax.broadcasted_iota(jnp.int32, (1, PAIR), 1)
    first = (lane < HD).astype(jnp.float32)
    return first.astype(dtype), (1.0 - first).astype(dtype)


def gather_blocks(nb_ref, kv_refs, kv_s, rows):
    far = jnp.maximum(nb_ref[0], nb_ref[1] - 1)
    for e in range(CHIPS):
        low = (SPOTS - 2 - 2 * e) * rows

        def fill(e=e, low=low):
            kv_s[:, low : low + 2 * rows, :] = kv_refs[e][...]

        if e == 0:
            fill()
        else:
            pl.when(far >= 2 * e - 1)(fill)


def forward_kernel(nb_ref, q_ref, *refs):
    kv_refs = refs[:CHIPS]
    lo_ref, hi_ref, code_ref, o_ref, lse_ref, kv_s = refs[CHIPS:]
    rows = q_ref.shape[0] // 2
    gather_blocks(nb_ref, kv_refs, kv_s, rows)
    first, second = halves(jnp.bfloat16)
    first_f, second_f = halves(jnp.float32)
    for qb in range(2):
        q = q_ref[qb * rows : (qb + 1) * rows, :]
        q_heads = (q * first, q * second)
        lo, hi = lo_ref[qb], hi_ref[qb]

        def tile(d, carry, q_heads=q_heads, lo=lo, hi=hi, qb=qb):
            tops, totals, acc = carry
            spot = SPOTS - 2 + qb - d
            at = pl.ds(pl.multiple_of(spot * rows, rows), rows)
            k, v = kv_s[0, at, :], kv_s[1, at, :]
            code = code_ref[spot]
            ok = (code >= lo) & (code <= hi)
            new_tops, new_totals, decays = [], [], []
            gain = None
            for h, v_mask in enumerate((first, second)):
                s = jnp.where(ok, times_transposed(q_heads[h], k), masked_out)
                top = jnp.maximum(tops[h], jnp.max(s, axis=1, keepdims=True))
                p = jnp.exp(s - top)
                decay = jnp.exp(tops[h] - top)
                new_tops.append(top)
                new_totals.append(totals[h] * decay + jnp.sum(p, axis=1, keepdims=True))
                decays.append(decay)
                part = matmul(p.astype(jnp.bfloat16), v * v_mask)
                gain = part if gain is None else gain + part
            acc = acc * (decays[0] * first_f + decays[1] * second_f) + gain
            return tuple(new_tops), tuple(new_totals), acc

        start = jnp.full((rows, 1), masked_out, jnp.float32)
        none = jnp.zeros((rows, 1), jnp.float32)
        tops, totals, acc = lax.fori_loop(
            0,
            nb_ref[qb] + 1,
            tile,
            ((start, start), (none, none), jnp.zeros((rows, PAIR), jnp.float32)),
        )
        here = slice(qb * rows, (qb + 1) * rows)
        o_ref[here, :] = acc / (totals[0] * first_f + totals[1] * second_f)
        lse = [tops[h] + jnp.log(totals[h]) for h in range(2)]
        lse_ref[here, :] = lse[0] * first_f + lse[1] * second_f


def backward_kernel(nb_ref, q_ref, do_ref, *refs):
    kv_refs = refs[:CHIPS]
    lo_ref, hi_ref, code_ref, stat_ref, dq_ref, dkv_ref, kv_s, dk_s, dv_s = refs[CHIPS:]
    rows = q_ref.shape[0] // 2
    gather_blocks(nb_ref, kv_refs, kv_s, rows)
    dk_s[...] = jnp.zeros_like(dk_s)
    dv_s[...] = jnp.zeros_like(dv_s)
    first, second = halves(jnp.bfloat16)
    for qb in range(2):
        here = slice(qb * rows, (qb + 1) * rows)
        q, do = q_ref[here, :], do_ref[here, :]
        q_heads = (q * first, q * second)
        do_heads = (do * first, do * second)
        lo, hi = lo_ref[qb], hi_ref[qb]

        def tile(d, dq_parts, q_heads=q_heads, do_heads=do_heads, lo=lo, hi=hi, qb=qb, here=here):
            spot = SPOTS - 2 + qb - d
            at = pl.ds(pl.multiple_of(spot * rows, rows), rows)
            k, v = kv_s[0, at, :], kv_s[1, at, :]
            k_turned = k.astype(jnp.float32).T.astype(jnp.bfloat16)
            code = code_ref[spot]
            ok = (code >= lo) & (code <= hi)
            new_parts = []
            dk = dv = None
            for h in range(2):
                s = times_transposed(k, q_heads[h])
                p = jnp.where(ok, jnp.exp(s - stat_ref[h : h + 1, here]), 0.0)
                dp = times_transposed(v, do_heads[h])
                ds = (p * (dp - stat_ref[2 + h : 3 + h, here])).astype(jnp.bfloat16)
                dv_part = matmul(p.astype(jnp.bfloat16), do_heads[h])
                dk_part = matmul(ds, q_heads[h])
                dv = dv_part if dv is None else dv + dv_part
                dk = dk_part if dk is None else dk + dk_part
                new_parts.append(dq_parts[h] + matmul(k_turned[h * HD : (h + 1) * HD, :], ds))
            dk_s[at, :] += dk
            dv_s[at, :] += dv
            return tuple(new_parts)

        none = jnp.zeros((HD, rows), jnp.float32)
        parts = lax.fori_loop(0, nb_ref[qb] + 1, tile, (none, none))
        turned = jnp.concatenate(parts, axis=0).T
        dq_ref[here, :] = (turned * HD ** (-0.5)).astype(jnp.bfloat16)
    for e in range(CHIPS):
        low = (SPOTS - 2 - 2 * e) * rows
        dkv_ref[e, 0] = dk_s[low : low + 2 * rows, :].astype(jnp.bfloat16)
        dkv_ref[e, 1] = dv_s[low : low + 2 * rows, :].astype(jnp.bfloat16)


def specs(count):
    return [pl.BlockSpec(memory_space=pltpu.SMEM)] + [pl.BlockSpec(memory_space=pltpu.VMEM)] * (
        count - 1
    )


def attend(nb, q, kvs, lo, hi, code):
    both = q.shape[0]
    operands = (nb, q, *kvs, lo, hi, code)
    out = jax.ShapeDtypeStruct((both, PAIR), jnp.float32)
    return pl.pallas_call(
        forward_kernel,
        out_shape=(out, out),
        in_specs=specs(len(operands)),
        out_specs=(pl.BlockSpec(memory_space=pltpu.VMEM),) * 2,
        scratch_shapes=[pltpu.VMEM((2, CHIPS * both, PAIR), jnp.bfloat16)],
        compiler_params=pltpu.CompilerParams(vmem_limit_bytes=VMEM_LIMIT),
        cost_estimate=pl.CostEstimate(
            flops=8 * both * both * 3 * PAIR, bytes_accessed=8 * both * PAIR * 4, transcendentals=0
        ),
        name="attend",
    )(*operands)


def attend_back(nb, q, do, kvs, lo, hi, code, stats):
    both = q.shape[0]
    operands = (nb, q, do, *kvs, lo, hi, code, stats)
    return pl.pallas_call(
        backward_kernel,
        out_shape=(
            jax.ShapeDtypeStruct((both, PAIR), jnp.bfloat16),
            jax.ShapeDtypeStruct((CHIPS, 2, both, PAIR), jnp.bfloat16),
        ),
        in_specs=specs(len(operands)),
        out_specs=(pl.BlockSpec(memory_space=pltpu.VMEM),) * 2,
        scratch_shapes=[
            pltpu.VMEM((2, CHIPS * both, PAIR), jnp.bfloat16),
            pltpu.VMEM((CHIPS * both, PAIR), jnp.float32),
            pltpu.VMEM((CHIPS * both, PAIR), jnp.float32),
        ],
        compiler_params=pltpu.CompilerParams(vmem_limit_bytes=VMEM_LIMIT),
        cost_estimate=pl.CostEstimate(
            flops=20 * both * both * 3 * PAIR, bytes_accessed=16 * both * PAIR * 4, transcendentals=0
        ),
        name="attend_back",
    )(*operands)


def doubled(held, device):
    levels = lax.axis_size("fsdp").bit_length() - 1
    for bit in range(levels):
        other = swap(held, bit)
        own = (device >> bit) & 1
        low = jnp.where(own == 0, held, other)
        high = jnp.where(own == 0, other, held)
        held = jnp.concatenate([low, high], axis=0)
    return held


def owner_sums(grads, device, order, sent_as=jnp.bfloat16):
    peers = lax.axis_size("fsdp")
    levels = peers.bit_length() - 1
    width = grads.shape[1]
    held = grads.reshape((2,) * levels + (grads.shape[0] // peers, width))
    left = list(range(levels - 1, -1, -1))
    for bit in list(order) + list(range(len(order), levels)):
        axis = left.index(bit)
        own = (device >> bit) & 1
        sent = lax.dynamic_index_in_dim(held, 1 - own, axis, keepdims=False)
        kept = lax.dynamic_index_in_dim(held, own, axis, keepdims=False)
        held = kept + swap(sent.astype(sent_as), bit).astype(jnp.float32)
        left.pop(axis)
    return held


def per_device(
    tokens,
    lengths,
    counts,
    ln1_gain,
    ln1_bias,
    w_qkv,
    bias_q,
    bias_v,
    w_out,
    bias_out,
    ln2_gain,
    ln2_bias,
    w_fc,
    bias_fc,
    w_proj,
    bias_proj,
    grad_out,
):
    rows, features = tokens.shape
    half = features // 2
    pair_count = half // PAIR
    peers = lax.axis_size("fsdp")
    device = lax.axis_index("fsdp")
    core = device % 2

    small_parts = (
        ln1_gain, ln1_bias, bias_q, bias_v, bias_out, ln2_gain, ln2_bias, bias_proj, bias_fc,
    )
    sizes = [part.shape[0] for part in small_parts]
    packed = jnp.concatenate(small_parts).reshape(1, -1)
    packed_all = doubled(packed.astype(jnp.float32), device)
    weight_qkv = lax.all_gather(w_qkv, "fsdp", axis=0, tiled=True)
    weight_out = lax.all_gather(w_out, "fsdp", axis=0, tiled=True)
    weight_fc = lax.all_gather(w_fc, "fsdp", axis=0, tiled=True)
    weight_proj = lax.all_gather(w_proj, "fsdp", axis=0, tiled=True)
    whole, at = [], 0
    for size in sizes:
        whole.append(packed_all[:, at : at + size].reshape(-1))
        at += size
    (
        gain_one, shift_one, query_bias, value_bias, out_bias, gain_two, shift_two, proj_bias, fc_bias,
    ) = whole

    seq_ends = jnp.cumsum(lengths)
    seq_starts = seq_ends - lengths
    starts = jnp.cumsum(counts) - counts
    offsets = jnp.arange(rows, dtype=jnp.int32)
    total_slots = peers * rows

    def begin_of(places):
        passed = places[..., None] >= seq_ends
        nearest = jnp.max(jnp.where(passed, seq_ends, 0), axis=-1)
        return nearest

    def codes_of(owners):
        safe = jnp.clip(owners, 0, peers - 1)
        places = starts[safe][:, None] + offsets[None, :]
        alive = offsets[None, :] < counts[safe][:, None]
        blank = total_slots + safe[:, None] * rows + offsets[None, :]
        codes = jnp.where(alive, places, blank)
        return codes, jnp.where(alive, begin_of(places), blank)

    first_device = device - core
    near = first_device + jnp.arange(2, dtype=jnp.int32)
    around = first_device - (SPOTS - 2) + jnp.arange(SPOTS, dtype=jnp.int32)
    key_codes = codes_of(around)[0]
    hi, lo = codes_of(near)
    earliest = begin_of(starts[near])
    back = near[:, None] - jnp.arange(1, REACH + 1, dtype=jnp.int32)[None, :]
    back_safe = jnp.clip(back, 0, peers - 1)
    seen = (back >= 0) & (starts[back_safe] + counts[back_safe] > earliest[:, None])
    nb = jnp.sum(seen.astype(jnp.int32), axis=1)
    lo_col, hi_col, code_row = lo[:, :, None], hi[:, :, None], key_codes[:, None, :]
    lo_row, hi_row, code_col = lo[:, None, :], hi[:, None, :], key_codes[:, :, None]

    def trade(x):
        n = x.shape[0]
        cut = x.reshape(n, rows, 2, half)
        mine = lax.dynamic_index_in_dim(cut, core, 2, keepdims=False)
        other = swap(lax.dynamic_index_in_dim(cut, 1 - core, 2, keepdims=False), 0)
        low = jnp.where(core == 0, mine, other)
        high = jnp.where(core == 0, other, mine)
        return jnp.concatenate([low, high], axis=1)

    def trade_back(x):
        mine = lax.dynamic_slice_in_dim(x, core * rows, rows, 1)
        other = swap(lax.dynamic_slice_in_dim(x, (1 - core) * rows, rows, 1), 0)
        low = jnp.where(core == 0, mine, other)
        high = jnp.where(core == 0, other, mine)
        return jnp.concatenate([low, high], axis=2)

    live = (offsets < counts[device])[:, None]
    inputs = tokens.astype(jnp.float32)
    normed_low = layer_norm(inputs, gain_one, shift_one).astype(jnp.bfloat16)
    projected = matmul(normed_low, weight_qkv)
    query = (projected[:, :features] + query_bias).astype(jnp.bfloat16) * jnp.bfloat16(HD ** (-0.5))
    keys = projected[:, features : 2 * features].astype(jnp.bfloat16)
    vals = (projected[:, 2 * features :] + value_bias).astype(jnp.bfloat16)
    traded = trade(jnp.stack([query, keys, vals]))
    queries, blocks, outs, lses = [], [], [], []
    for pair in range(pair_count):
        columns = slice(pair * PAIR, (pair + 1) * PAIR)
        own = traded[1:, :, columns]
        queries.append(traded[0, :, columns])
        blocks.append([own] + [from_behind(own, 2 * e) for e in range(1, CHIPS)])
    for pair in range(pair_count):
        out, lse = attend(nb, queries[pair], blocks[pair], lo_col, hi_col, code_row)
        outs.append(out)
        lses.append(lse)
    attended = jnp.concatenate(outs, axis=1)
    mixed_low = trade_back(attended.astype(jnp.bfloat16)[None])[0]
    middle = inputs + matmul(mixed_low, weight_out) + out_bias
    two_low = layer_norm(middle, gain_two, shift_two).astype(jnp.bfloat16)
    hidden = matmul(two_low, weight_fc) + fc_bias
    active, gelu_back = jax.vjp(smooth_gelu, hidden)
    active_low = active.astype(jnp.bfloat16)
    result = middle + matmul(active_low, weight_proj) + proj_bias
    activations = jnp.where(live, result, 0.0).astype(jnp.bfloat16)

    upstream = jnp.where(live, grad_out.astype(jnp.float32), 0.0)
    upstream_low = upstream.astype(jnp.bfloat16)
    grad_w_proj = transposed_times(active_low, upstream_low)
    grad_bias_proj = jnp.sum(upstream, axis=0)
    d_active = times_transposed(upstream_low, weight_proj)
    d_hidden = gelu_back(d_active)[0].astype(jnp.bfloat16)
    grad_w_fc = transposed_times(two_low, d_hidden)
    grad_bias_fc = column_sums(d_hidden)
    d_normed_two = times_transposed(d_hidden, weight_fc)
    unused_two, norm_back_two = jax.vjp(layer_norm, middle, gain_two, shift_two)
    d_middle_part, grad_ln2_gain, grad_ln2_bias = norm_back_two(d_normed_two)
    d_middle = upstream + d_middle_part
    d_branch = d_middle.astype(jnp.bfloat16)
    grad_w_out = transposed_times(mixed_low, d_branch)
    grad_bias_out = column_sums(d_branch)
    d_attended = trade(times_transposed(d_branch, weight_out).astype(jnp.bfloat16)[None])[0]

    own_proj = owner_sums(grad_w_proj, device, (0, 1, 2))
    own_fc = owner_sums(grad_w_fc, device, (0, 2, 1))
    own_out = owner_sums(grad_w_out, device, (0, 2, 1))

    d_queries, d_pairs = [], []
    for pair in range(pair_count):
        columns = slice(pair * PAIR, (pair + 1) * PAIR)
        d_out = d_attended[:, columns]
        products = d_out.astype(jnp.float32) * outs[pair]
        delta = jnp.sum(products.reshape(2 * rows, 2, HD), axis=2)
        stats = jnp.concatenate([lses[pair][:, ::HD].T, delta.T], axis=0)
        d_query, d_blocks = attend_back(
            nb, queries[pair], d_out, blocks[pair], lo_row, hi_row, code_col, stats
        )
        total = d_blocks[0].astype(jnp.float32)
        for e in range(1, CHIPS):
            total = total + from_behind(d_blocks[e], -2 * e).astype(jnp.float32)
        d_queries.append(d_query)
        d_pairs.append(total.astype(jnp.bfloat16))
    d_heads = jnp.concatenate(
        [jnp.concatenate(d_queries, axis=1)[None], jnp.concatenate(d_pairs, axis=2)], axis=0
    )
    d_slots = trade_back(d_heads)
    d_projected = jnp.concatenate([d_slots[0], d_slots[1], d_slots[2]], axis=1)
    grad_w_qkv = transposed_times(normed_low, d_projected)
    middle_column = grad_w_qkv.shape[1] // 2
    own_qkv = jnp.concatenate(
        [
            owner_sums(grad_w_qkv[:, :middle_column], device, (0, 1, 2)),
            owner_sums(grad_w_qkv[:, middle_column:], device, (0, 2, 1)),
        ],
        axis=1,
    )
    grad_bias_q = column_sums(d_slots[0])
    grad_bias_v = column_sums(d_slots[2])
    d_normed_one = times_transposed(d_projected, weight_qkv)
    unused_one, norm_back_one = jax.vjp(layer_norm, inputs, gain_one, shift_one)
    d_input_part, grad_ln1_gain, grad_ln1_bias = norm_back_one(d_normed_one)
    grad_tokens = (d_middle + d_input_part).astype(jnp.bfloat16)

    small_grads = (
        grad_ln1_gain, grad_ln1_bias, grad_bias_q, grad_bias_v, grad_bias_out, grad_ln2_gain,
        grad_ln2_bias, grad_bias_proj, grad_bias_fc,
    )
    packed_grads = jnp.concatenate([g.reshape(peers, -1) for g in small_grads], axis=1)
    own_small = owner_sums(packed_grads, device, (0, 1, 2), jnp.float32)[0]
    small, at = [], 0
    for size in sizes:
        small.append(own_small[at : at + size])
        at += size
    (
        own_gain_one, own_shift_one, own_bias_q, own_bias_v, own_bias_out, own_gain_two,
        own_shift_two, own_bias_proj, own_bias_fc,
    ) = small
    return (
        activations,
        grad_tokens,
        own_gain_one,
        own_shift_one,
        own_qkv,
        own_bias_q,
        own_bias_v,
        own_out,
        own_bias_out,
        own_gain_two,
        own_shift_two,
        own_fc,
        own_bias_fc,
        own_proj,
        own_bias_proj,
    )


def solution(mesh):
    split_rows, split_flat = P("fsdp", None), P("fsdp")
    return jax.shard_map(
        per_device,
        mesh=mesh,
        in_specs=(
            split_rows, P(), P(),
            split_flat, split_flat, split_rows, split_flat, split_flat, split_rows, split_flat,
            split_flat, split_flat, split_rows, split_flat, split_rows, split_flat, split_rows,
        ),
        out_specs=(
            split_rows, split_rows,
            split_flat, split_flat, split_rows, split_flat, split_flat, split_rows, split_flat,
            split_flat, split_flat, split_rows, split_flat, split_rows, split_flat,
        ),
        check_vma=False,
    )
```
